1024 devices in a mesh: col: 64 (over x, z), row: 8 (over y), lev: 2 (over core).
Axes of the slice: x: 8, y: 8, z: 8, core: 2. Of those that a mesh axis runs over, the one named last changes fastest.
Arguments:
- state: float32 [2, 8, 512, 32768], P(None, 'lev', 'row', 'col'), may hold values from -6 to 6
- atm_flux: bfloat16 [8, 2, 3072, 512], P('row', 'lev', 'col'), may hold values from -6 to 6
- intersection: int32 [8, 2, 3072, 2], P('row', 'lev', 'col'), may hold values from 0 to 63, all different within a row; in each aligned block of 48 rows (0 to 47, 48 to 95, ..., all dimensions but the last counted through in order) at most 3 rows name the same one
- weight_index: int32 [8, 2, 3072, 2], P('row', 'lev', 'col'), may hold values from 0 to 23
- target_row: int32 [8, 2, 3072, 2], P('row', 'lev', 'col'), may hold values from 0 to 63
- remap_weights: bfloat16 [24, 128, 512], replicated, may hold values from -0.5 to 0.5
- land_mask: int32 [512, 32768], P('row', 'col'), may hold values 0 or 1
- profiles: float32 [3, 8], P(None, 'lev'), may hold values from 0.2 to 1
Outputs:
- final_state: float32 [2, 8, 512, 32768], P(None, 'lev', 'row', 'col')
The draws below stay inside these ranges and needn't reach their ends.
Inputs may be any that keep to these rules, and one draw needn't show every extreme that they name: `intersection`: the two partitions of one block differ; at most 3 of the blocks on one device name the same partition, and some device's blocks name one partition exactly 3 times.
All inputs are finite; a program needn't handle non-finite values. No bound on the sum of `land_mask` on one device may be relied on, other than what follows from the above.
Results may differ from the reference program's by a relative error of at most 0.00049.
Values may be sent and summed in bfloat16 or wider, within the bound.
A program may use at most 32 MiB of HBM per device.

```python
import math
import jax
import jax.numpy as jnp
import numpy as np
from jax import lax

AC = 128
NW = 24
STEPS = 4
ADEV = 48
OX = 512
OY = 64
CAP = 3
A_BLOCKS = 3072
NX = 32768
NY = 512
LEVELS = 8
N_COL = 64
N_ROW = 8
N_LEV = 2


def with_ends(entries, stream_key, smallest, high):
    place = [jax.random.randint(jax.random.fold_in(stream_key, axis), (), 0, length) for axis, length in enumerate(entries.shape)]
    widest = entries.shape.index(max(entries.shape))
    next_to = place[:widest] + [(place[widest] + 1) % entries.shape[widest]] + place[widest + 1:]
    return entries.at[tuple(place)].set(smallest).at[tuple(next_to)].set(high)


def block_scale(key, shape, cuts, smallest, largest):
    gain = 1.0
    for dim, parts in cuts:
        heights = jax.random.uniform(jax.random.fold_in(jax.random.fold_in(key, 6), dim), (parts,), jnp.float32, smallest / len(cuts), largest / len(cuts))
        gain = gain * jnp.repeat(jnp.exp(heights), shape[dim] // parts).reshape((-1,) + (1,) * (len(shape) - 1 - dim))
    return gain


def deal_out(key, own, number, rows, count, top, limit, skew):
    sequence = jax.random.permutation(key, count)
    crowded, usual = load_shares(count, rows * top, limit, skew, True), load_shares(count, rows * top, limit, skew, False)
    places = jnp.arange(count)

    def named(lengths, turn):
        used = int((lengths > 0).sum())
        fixed = max(1, used // 4)
        shifted = fixed + (places - fixed + turn * (used - fixed)) % max(1, count - fixed)
        return jnp.zeros((count,), jnp.int32).at[sequence[jnp.where(places < fixed, places, shifted)]].set(jnp.asarray(lengths, jnp.int32))

    lengths = jnp.where(number % 4 == 0, named(crowded, number // 4), named(usual, number - number // 4 - 1))
    mixed = jax.random.permutation(jax.random.fold_in(own, 3), count)
    giver, receiver = mixed[0:count // 2 * 2:2], mixed[1:count // 2 * 2:2]
    slack = jnp.minimum(lengths[giver] - 1, limit - lengths[receiver]) // 2
    slack = jnp.where((giver == sequence[0]) | (receiver == sequence[0]) | (lengths[receiver] == 0), 0, jnp.maximum(slack, 0))
    shifted = jax.random.randint(jax.random.fold_in(own, 4), (count // 2,), 0, 1 << 20) % (slack + 1)
    lengths = lengths.at[giver].add(-shifted).at[receiver].add(shifted)
    labels = jnp.searchsorted(jnp.cumsum(lengths), jnp.arange(rows * top), side="right").astype(jnp.int32)
    table = labels.reshape(top, rows).T
    table = table[jax.random.permutation(jax.random.fold_in(own, 1), rows)]
    turn = jax.random.randint(jax.random.fold_in(own, 2), (rows, 1), 0, top)
    return jnp.take_along_axis(table, (jnp.arange(top)[None, :] + turn) % top, axis=1)


def load_shares(amount, total, limit, slope, full):
    portions = [(1 << 20) // math.isqrt(grade ** slope) + 1 for grade in range(1, amount + 1)]
    largest = limit if full else min(limit, max(-(-total // amount), total * portions[0] // sum(portions)))
    least = 1 if total - largest >= amount - 1 else 0
    holding, rest = [largest] + [least] * (amount - 1), total - largest - least * (amount - 1)
    while rest > 0:
        candidates = [i for i in range(1, amount) if holding[i] < largest] or [i for i in range(1, amount) if holding[i] < limit]
        whole, remaining = sum([portions[i] for i in candidates]), rest
        for i in candidates:
            addition = min(limit - holding[i], max(1, remaining * portions[i] // whole), rest)
            holding[i] = holding[i] + addition
            rest = rest - addition
    return np.array(holding)


def bell_draw(stream_key, shape, width, bound, pieces=(), kind=jnp.bfloat16):
    level = block_scale(stream_key, shape, pieces, -0.22, 0.18) if pieces else 1.0
    values = jax.random.normal(stream_key, shape, jnp.float32) * width * level
    return jnp.minimum(jnp.maximum(values, -bound), bound).astype(kind)


def setup_inputs(seed: int = 0) -> dict:
    key_list = jax.random.split(jax.random.key(seed), 9)
    state = bell_draw(key_list[0], (2, LEVELS, NY, NX), 1.0, 6.0, ((1, 2), (2, 8), (3, 64)), jnp.float32)
    atm_flux = bell_draw(key_list[1], (N_ROW, N_LEV, A_BLOCKS, 4 * AC), 1.0, 6.0, ((0, 8), (1, 2), (2, 64)))
    intersection_keys = jax.random.split(jax.random.fold_in(key_list[2], 1), N_ROW * N_LEV * A_BLOCKS // ADEV)
    intersection_turns = jax.random.permutation(jax.random.fold_in(key_list[2], 3), N_ROW * N_LEV * A_BLOCKS // ADEV)
    intersection = jax.vmap(lambda own, number: deal_out(jax.random.fold_in(key_list[2], 2), own, number, ADEV, N_COL, 2, CAP, 2))(intersection_keys, intersection_turns).reshape((N_ROW, N_LEV, A_BLOCKS, 2))
    weight_index = with_ends(jax.random.randint(key_list[3], (N_ROW, N_LEV, A_BLOCKS, 2), 0, NW), jax.random.fold_in(key_list[3], 1), 0, NW - 1).astype(jnp.int32)
    target_row = with_ends(jax.random.randint(key_list[4], (N_ROW, N_LEV, A_BLOCKS, 2), 0, OY), jax.random.fold_in(key_list[4], 1), 0, OY - 1).astype(jnp.int32)
    remap_weights = bell_draw(key_list[5], (NW, AC, OX), AC ** -0.5, 0.5)
    land_mask = with_ends((jax.random.randint(key_list[6], (NY, NX), 0, 5) < 4).astype(jnp.int32), jax.random.fold_in(key_list[6], 1), 0, 1)
    profiles = jnp.clip(jnp.exp(math.log(1.0) - 1.609438 * jax.random.uniform(key_list[7], (3, LEVELS), jnp.float32) ** block_scale(key_list[7], (3, LEVELS), ((1, 2),), -0.2, 0.2)), 0.2, 1.0)
    return {"state": state, "atm_flux": atm_flux, "intersection": intersection, "weight_index": weight_index, "target_row": target_row, "remap_weights": remap_weights, "land_mask": land_mask, "profiles": profiles}


DIFFUSE = 0.2
SPEED = 0.3
FORCE_STEP = 0.25


def advance(tracer, padded, east_speed, north_speed, source, wet):
    center = padded[..., 1:-1, 1:-1]
    east = padded[..., 1:-1, 2:]
    west = padded[..., 1:-1, :-2]
    north = padded[..., 2:, 1:-1]
    south = padded[..., :-2, 1:-1]
    fresh = center + DIFFUSE * (east + west + north + south - 4.0 * center)
    fresh = fresh - 0.5 * east_speed * (east - west) - 0.5 * north_speed * (north - south)
    fresh = fresh + FORCE_STEP * source
    return jnp.where(wet, fresh, tracer)


def reference(state, atm_flux, intersection, weight_index, target_row, remap_weights, land_mask, profiles):
    table = remap_weights.reshape(NW * AC, OX)

    def remap_band(inputs):
        flux_band, intersection_band, index_band, row_band = inputs
        total = jnp.zeros((4, OY, NX), jnp.float32)
        for substep in range(N_LEV):
            bins = ((intersection_band[substep] * OY + row_band[substep]) * NW + index_band[substep]).reshape(-1)
            pair_flux = jnp.repeat(flux_band[substep].astype(jnp.float32), 2, axis=0)
            grouped = jax.ops.segment_sum(pair_flux, bins.astype(jnp.int32), num_segments=N_COL * OY * NW)
            grouped = grouped.astype(jnp.bfloat16)
            rows = grouped.reshape(N_COL * OY, NW, 4, AC).transpose(0, 2, 1, 3).reshape(N_COL * OY * 4, NW * AC)
            part = jnp.dot(rows, table, preferred_element_type=jnp.float32)
            total = total + part.reshape(N_COL, OY, 4, OX).transpose(2, 1, 0, 3).reshape(4, OY, NX)
        return total

    bands = lax.map(remap_band, (atm_flux, intersection, weight_index, target_row))
    forcing = bands.transpose(1, 0, 2, 3).reshape(4, NY, NX)
    wet = land_mask == 1
    east_base = SPEED * jnp.tanh(forcing[2])
    north_base = SPEED * jnp.tanh(forcing[3])

    def one_level(inputs):
        tracer, weights = inputs
        east_speed = east_base * weights[2]
        north_speed = north_base * weights[2]
        source = jnp.stack([forcing[0] * weights[0], forcing[1] * weights[1]])
        for step in range(STEPS):
            padded = jnp.pad(tracer, ((0, 0), (1, 1), (1, 1)))
            tracer = advance(tracer, padded, east_speed, north_speed, source, wet)
        return tracer

    levels = lax.map(one_level, (state.transpose(1, 0, 2, 3), profiles.T))
    return levels.transpose(1, 0, 2, 3)
```

```python
import functools

import jax
import jax.numpy as jnp
from jax import lax
from jax.experimental import pallas as pl
from jax.experimental.pallas import tpu as pltpu
from jax.sharding import PartitionSpec as P

STEPS = 4
DIFFUSE = 0.2
SPEED = 0.3
FORCE_STEP = 0.25

MESH = pl.DeviceIdType.MESH
F32 = jnp.float32
BF16 = jnp.bfloat16
I32 = jnp.int32

CAP = 3
FIELDS = 4
SLOT = 64
ROWS = 64
WIDTH = 512
LANES = 128
BLOCKS = WIDTH // LANES
PAD = 8
EXT = ROWS + 2 * PAD
GROUP = EXT // 16
TILES = EXT * 8
HALO = STEPS


def row_of(ref, xb, r):
    return ref[xb, pl.ds(pl.multiple_of(r * 8, 8), 8), :]


def kernel(
    sizes,
    prof_ref,
    dest_ref,
    widx_ref,
    trow_ref,
    flux_ref,
    mask_ref,
    state_ref,
    weights_ref,
    out_ref,
    send,
    got,
    stage,
    wv,
    lhs,
    hot,
    slots,
    mine,
    theirs,
    nat,
    cells,
    force,
    coef,
    own,
    other,
    load_sem,
    out_sem,
    a2a_send,
    a2a_recv,
    lev_send,
    lev_recv,
    row_send,
    row_recv,
    col_send,
    col_recv,
):
    columns, bands = sizes
    col = lax.axis_index("col")
    row = lax.axis_index("row")
    lev = lax.axis_index("lev")
    west = lax.rem(col + columns - 1, columns)
    east = lax.rem(col + 1, columns)
    south = lax.rem(row + bands - 1, bands)
    north = lax.rem(row + 1, bands)

    state_copy = pltpu.make_async_copy(state_ref, nat, load_sem.at[0])
    weights_copy = pltpu.make_async_copy(weights_ref, wv, load_sem.at[1])
    state_copy.start()
    weights_copy.start()

    barrier = pltpu.get_barrier_semaphore()

    def greet(d, carry):
        pl.semaphore_signal(
            barrier, inc=1, device_id={"col": lax.rem(col + d, columns)}, device_id_type=MESH
        )
        return carry

    lax.fori_loop(1, columns, greet, 0)
    pl.semaphore_signal(barrier, inc=1, device_id={"row": south}, device_id_type=MESH)
    pl.semaphore_signal(barrier, inc=1, device_id={"row": north}, device_id_type=MESH)
    pl.semaphore_signal(barrier, inc=1, device_id={"lev": 1 - lev}, device_id_type=MESH)

    blocks = dest_ref.shape[1]
    dest = dest_ref[...]
    to = lax.broadcasted_iota(I32, (columns, blocks), 0)
    first = dest[0:1, :] == to
    second = dest[1:2, :] == to
    named = (first | second).astype(F32)
    before = (
        lax.broadcasted_iota(I32, (blocks, blocks), 0)
        < lax.broadcasted_iota(I32, (blocks, blocks), 1)
    ).astype(F32)
    rank = jnp.dot(named.astype(BF16), before.astype(BF16), preferred_element_type=F32)
    y_one = jnp.where(first, trow_ref[0:1, :], trow_ref[1:2, :]).astype(F32) + 1.0
    w_val = jnp.where(first, widx_ref[0:1, :], widx_ref[1:2, :]).astype(F32)
    spot = lax.broadcasted_iota(I32, (blocks, LANES), 1)
    at_y = (spot == col).astype(BF16)
    at_w = (spot == col + SLOT).astype(BF16)
    flux = flux_ref[...]
    for k in range(CAP):
        pick = jnp.where(rank == float(k), named, 0.0)
        moved = jnp.dot(pick.astype(BF16), flux, preferred_element_type=F32)
        for f in range(FIELDS):
            stage[pl.ds(k * FIELDS + f, columns, stride=16), :] = moved[:, f * LANES : (f + 1) * LANES]
        tags = jnp.dot((pick * y_one).astype(BF16), at_y, preferred_element_type=F32) + jnp.dot(
            (pick * w_val).astype(BF16), at_w, preferred_element_type=F32
        )
        stage[pl.ds(CAP * FIELDS + k, columns, stride=16), :] = tags
    stage[pl.ds(15, columns, stride=16), :] = jnp.zeros((columns, LANES), F32)
    send[...] = stage[...].astype(BF16).reshape(columns, 16, LANES)

    pl.semaphore_wait(barrier, columns + 2)

    def push(d, carry):
        target = lax.rem(col + d, columns)
        pltpu.make_async_remote_copy(
            src_ref=send.at[target],
            dst_ref=got.at[col],
            send_sem=a2a_send,
            recv_sem=a2a_recv,
            device_id={"col": target},
            device_id_type=MESH,
        ).start()
        return carry

    lax.fori_loop(1, columns, push, 0)
    got[pl.ds(col, 1)] = send[pl.ds(col, 1)]

    zero_rows = jnp.zeros((BLOCKS, PAD * 8, LANES), F32)
    spare = (PAD - HALO) * 8
    for ref in (cells.at[0], force):
        ref[:, 0:spare, :] = zero_rows[:, :spare]
        ref[:, TILES - spare : TILES, :] = zero_rows[:, :spare]
    state_copy.wait()
    for xb in range(BLOCKS):
        for t in range(8):
            cells[0, xb, pl.ds(PAD * 8 + t, ROWS, stride=8), :] = nat[t, :, xb * LANES : (xb + 1) * LANES]

    def row_copies(ref, tag, count):
        rows = count * 8
        to_north = pltpu.make_async_remote_copy(
            src_ref=ref.at[:, pl.ds((PAD + ROWS) * 8 - rows, rows), :],
            dst_ref=ref.at[:, pl.ds(PAD * 8 - rows, rows), :],
            send_sem=row_send.at[2 * tag],
            recv_sem=row_recv.at[2 * tag],
            device_id={"row": north},
            device_id_type=MESH,
        )
        to_south = pltpu.make_async_remote_copy(
            src_ref=ref.at[:, pl.ds(PAD * 8, rows), :],
            dst_ref=ref.at[:, pl.ds((PAD + ROWS) * 8, rows), :],
            send_sem=row_send.at[2 * tag + 1],
            recv_sem=row_recv.at[2 * tag + 1],
            device_id={"row": south},
            device_id_type=MESH,
        )
        return to_north, to_south

    def settle_rows(ref, copies):
        for copy in copies:
            copy.wait()

        @pl.when(row == 0)
        def _():
            ref[:, 0 : PAD * 8, :] = zero_rows

        @pl.when(row == bands - 1)
        def _():
            ref[:, (PAD + ROWS) * 8 : TILES, :] = zero_rows

    group = lax.broadcasted_iota(I32, (8, LANES), 1) // 8

    def pack(ref, tag):
        def one(j, carry):
            left = row_of(ref, 0, j)
            right = pltpu.roll(row_of(ref, BLOCKS - 1, j), 8, 1)
            for g in range(1, 16):
                r = g * GROUP + j
                left = jnp.where(group == g, pltpu.roll(row_of(ref, 0, r), 8 * g, 1), left)
                turned = row_of(ref, BLOCKS - 1, r)
                if g < 15:
                    turned = pltpu.roll(turned, 8 * g + 8, 1)
                right = jnp.where(group == g, turned, right)
            own[tag, 0, j] = left
            own[tag, 1, j] = right
            return carry

        lax.fori_loop(0, GROUP, one, 0)

    def col_copies(tag):
        to_west = pltpu.make_async_remote_copy(
            src_ref=own.at[tag, 0],
            dst_ref=other.at[tag, 1],
            send_sem=col_send.at[2 * tag],
            recv_sem=col_recv.at[2 * tag],
            device_id={"col": west},
            device_id_type=MESH,
        )
        to_east = pltpu.make_async_remote_copy(
            src_ref=own.at[tag, 1],
            dst_ref=other.at[tag, 0],
            send_sem=col_send.at[2 * tag + 1],
            recv_sem=col_recv.at[2 * tag + 1],
            device_id={"col": east},
            device_id_type=MESH,
        )
        return to_west, to_east

    def settle_cols(tag, copies):
        for copy in copies:
            copy.wait()

        @pl.when(col == 0)
        def _():
            other[tag, 0] = jnp.zeros((GROUP, 8, LANES), F32)

        @pl.when(col == columns - 1)
        def _():
            other[tag, 1] = jnp.zeros((GROUP, 8, LANES), F32)

    state_rows = row_copies(cells.at[0], 0, HALO)
    for copy in state_rows:
        copy.start()
    settle_rows(cells.at[0], state_rows)
    pack(cells.at[0], 0)
    state_cols = col_copies(0)
    for copy in state_cols:
        copy.start()
    settle_cols(0, state_cols)

    everyone = pltpu.make_async_remote_copy(
        src_ref=send.at[pl.ds(0, columns - 1)],
        dst_ref=got.at[pl.ds(0, columns - 1)],
        send_sem=a2a_send,
        recv_sem=a2a_recv,
        device_id={"col": east},
        device_id_type=MESH,
    )
    everyone.wait_recv()
    stage[...] = got[...].reshape(columns * 16, LANES).astype(F32)
    lane = lax.broadcasted_iota(I32, (1, LANES), 1)
    slots[...] = jnp.zeros_like(slots)
    bins = []
    for k in range(CAP):
        for f in range(FIELDS):
            slots[k * SLOT : k * SLOT + columns, f * LANES : (f + 1) * LANES] = stage[
                pl.ds(k * FIELDS + f, columns, stride=16), :
            ].astype(BF16)
        tags = jnp.sum(stage[pl.ds(CAP * FIELDS + k, columns, stride=16), :], axis=0, keepdims=True)
        y = tags.astype(I32) - 1
        w = pltpu.roll(tags, SLOT, 1).astype(I32)
        bins.append(jnp.where((y >= 0) & (lane < SLOT), w * ROWS + y, -1))
    low = jnp.where(lane < SLOT, bins[0], pltpu.roll(bins[1], SLOT, 1))
    bin_row = jnp.concatenate([low, bins[2]], axis=1)
    kinds = lhs.shape[1] // LANES
    batch = kinds * ROWS // 3
    for part in range(3):
        index = lax.broadcasted_iota(I32, (batch, 2 * LANES), 0) + part * batch
        hot[...] = jnp.where(index == bin_row, 1.0, 0.0).astype(BF16)
        summed = jnp.dot(hot[...], slots[...], preferred_element_type=F32).astype(BF16)
        for i in range(batch // ROWS):
            w = part * (batch // ROWS) + i
            for f in range(FIELDS):
                lhs[f * ROWS : (f + 1) * ROWS, w * LANES : (w + 1) * LANES] = summed[
                    i * ROWS : (i + 1) * ROWS, f * LANES : (f + 1) * LANES
                ]
    weights_copy.wait()
    swaps = []
    for half in range(2):
        mine[half] = jnp.dot(
            lhs[...], wv[:, half * 256 : (half + 1) * 256], preferred_element_type=F32
        )
        swap = pltpu.make_async_remote_copy(
            src_ref=mine.at[half],
            dst_ref=theirs.at[half],
            send_sem=lev_send.at[half],
            recv_sem=lev_recv.at[half],
            device_id={"lev": 1 - lev},
            device_id_type=MESH,
        )
        swap.start()
        swaps.append(swap)

    for half in range(2):
        swaps[half].wait()
        for inner in range(2):
            xb = 2 * half + inner
            here = slice(inner * LANES, (inner + 1) * LANES)
            wet = mask_ref[:, xb * LANES : (xb + 1) * LANES] == 1
            total = [
                mine[half, f * ROWS : (f + 1) * ROWS, here]
                + theirs[half, f * ROWS : (f + 1) * ROWS, here]
                for f in range(FIELDS)
            ]
            terms = [
                FORCE_STEP * total[0],
                FORCE_STEP * total[1],
                (0.5 * SPEED) * jnp.tanh(total[2]),
                (0.5 * SPEED) * jnp.tanh(total[3]),
                jnp.full((ROWS, LANES), DIFFUSE, F32),
            ]
            for f, term in enumerate(terms):
                force[xb, pl.ds(PAD * 8 + f, ROWS, stride=8), :] = jnp.where(wet, term, 0.0)
            for f in range(len(terms), 8):
                force[xb, pl.ds(PAD * 8 + f, ROWS, stride=8), :] = jnp.zeros((ROWS, LANES), F32)
    force_rows = row_copies(force, 1, HALO)
    for copy in force_rows:
        copy.start()

    tracer = lax.broadcasted_iota(I32, (8, LANES), 0)

    def profile(index, keep):
        value = jnp.zeros((8, LANES), F32)
        for level in range(4):
            value = jnp.where(
                (lax.rem(tracer, 4) == level) & keep, prof_ref[index, level], value
            )
        return value

    heat = profile(0, tracer < 4)
    fresh = profile(1, tracer >= 4)
    decay = profile(2, tracer >= 0)

    def factors(term):
        spread = [jnp.broadcast_to(term(f), (8, LANES)) for f in range(5)]
        source = spread[0] * heat + spread[1] * fresh
        a = spread[2] * decay
        b = spread[3] * decay
        d = spread[4]
        return 1.0 - 4.0 * d, d - a, d + a, d - b, d + b, source

    lanes = lax.broadcasted_iota(I32, (8, LANES), 1)

    def sides(cur):
        back = [pltpu.roll(c, 1, 1) for c in cur]
        ahead = [pltpu.roll(c, LANES - 1, 1) for c in cur]
        from_west = [jnp.where(lanes == 0, back[xb - 1], back[xb]) for xb in range(BLOCKS)]
        from_east = [
            jnp.where(lanes == LANES - 1, ahead[(xb + 1) % BLOCKS], ahead[xb])
            for xb in range(BLOCKS)
        ]
        return from_west, from_east

    def combine(c, below, cur, above, left, right):
        return (
            (c[0] * cur + c[5]) + (c[1] * right + c[2] * left) + (c[3] * above + c[4] * below)
        )

    def advance_row(step, r, below, cur, make):
        above = [row_of(cells.at[step], xb, r + 1) for xb in range(BLOCKS)]
        left, right = sides(cur)
        at = pl.ds(pl.multiple_of(r * 8, 8), 8)
        for xb in range(BLOCKS):
            if make:
                c = factors(lambda f: force[xb, pl.ds(r * 8 + f, 1), :])
                for i in range(6):
                    coef[i, xb, at, :] = c[i]
            else:
                c = [coef[i, xb, at, :] for i in range(6)]
            cells[step + 1, xb, at, :] = combine(c, below[xb], cur[xb], above[xb], left[xb], right[xb])
        return cur, above

    def sweep(step, low_row, count, make, unroll):
        below = [row_of(cells.at[step], xb, low_row - 1) for xb in range(BLOCKS)]
        cur = [row_of(cells.at[step], xb, low_row) for xb in range(BLOCKS)]

        def body(i, carry):
            below, cur = list(carry[:BLOCKS]), list(carry[BLOCKS:])
            for u in range(unroll):
                below, cur = advance_row(step, low_row + i * unroll + u, below, cur, make)
            return (*below, *cur)

        lax.fori_loop(0, count // unroll, body, (*below, *cur))

    sweep(0, PAD, ROWS, True, 2)
    settle_rows(force, force_rows)
    pack(force, 1)
    force_cols = col_copies(1)
    for copy in force_cols:
        copy.start()
    for step in range(1, STEPS):
        sweep(step, PAD + step, ROWS - 2 * step, False, 2)
    for step in range(STEPS):
        reach = STEPS - 1 - step
        for base in (PAD - reach, PAD + ROWS - step):
            below = [row_of(cells.at[step], xb, base - 1) for xb in range(BLOCKS)]
            cur = [row_of(cells.at[step], xb, base) for xb in range(BLOCKS)]
            for r in range(base, base + STEPS - 1):
                below, cur = advance_row(step, r, below, cur, step == 0)
    settle_cols(1, force_cols)

    spot8 = lax.rem(lax.broadcasted_iota(I32, (GROUP, 8, LANES), 2), 8)

    def strip_factors(ref):
        parts = [factors(lambda f: ref[j, f : f + 1, :]) for j in range(GROUP)]
        return [jnp.stack([p[i] for p in parts]) for i in range(6)]

    def turn(x, shift):
        return pltpu.roll(x, shift % LANES, 2)

    def strip(lefts, rights):
        (l_cells, l_force), (r_cells, r_force) = lefts, rights
        pair = [l_cells[...], r_cells[...]]
        cs = [strip_factors(l_force), strip_factors(r_force)]
        for _ in range(STEPS):
            rolled = []
            for side in range(2):
                x = pair[side]
                above = jnp.concatenate([x[1:], turn(x[:1], -8)], axis=0)
                below = jnp.concatenate([turn(x[-1:], 8), x[:-1]], axis=0)
                right, left = turn(x, -1), turn(x, 1)
                if side == 0:
                    right = jnp.where(spot8 == 7, turn(pair[1], 7), right)
                else:
                    left = jnp.where(spot8 == 0, turn(pair[0], -7), left)
                rolled.append(combine(cs[side], below, x, above, left, right))
            pair = rolled
        return pair

    own[0, 0] = strip((other.at[0, 0], other.at[1, 0]), (own.at[0, 0], own.at[1, 0]))[1]
    own[0, 1] = strip((own.at[0, 1], own.at[1, 1]), (other.at[0, 1], other.at[1, 1]))[0]
    last = cells.at[STEPS]
    for r in range(PAD, PAD + ROWS):
        g, j = r // GROUP, r % GROUP
        at = pl.ds(r * 8, 8)
        last[0, at, :] = jnp.where(lanes < 4, pltpu.roll(own[0, 0, j], (LANES - 8 * g) % LANES, 1), last[0, at, :])
        last[BLOCKS - 1, at, :] = jnp.where(
            lanes >= LANES - 4,
            pltpu.roll(own[0, 1, j], (LANES - 8 - 8 * g) % LANES, 1),
            last[BLOCKS - 1, at, :],
        )
    for t in range(8):
        for xb in range(BLOCKS):
            nat[t, :, xb * LANES : (xb + 1) * LANES] = last[xb, pl.ds(PAD * 8 + t, ROWS, stride=8), :]
    result = pltpu.make_async_copy(nat, out_ref, out_sem)
    result.start()
    result.wait()
    everyone.wait_send()


def local(
    state, atm_flux, intersection, weight_index, target_row, remap_weights, land_mask, profiles
):
    columns, bands = lax.axis_size("col"), lax.axis_size("row")
    per_device = atm_flux.shape[2]
    kinds, cells, width = remap_weights.shape

    def lists(x):
        return x.reshape(per_device, 2).T

    vmem = pl.BlockSpec(memory_space=pltpu.VMEM)
    hbm = pl.BlockSpec(memory_space=pl.ANY)
    dma = pltpu.SemaphoreType.DMA
    out = pl.pallas_call(
        functools.partial(kernel, (columns, bands)),
        out_shape=jax.ShapeDtypeStruct((8, ROWS, WIDTH), F32),
        in_specs=[pl.BlockSpec(memory_space=pltpu.SMEM)] + [vmem] * 5 + [hbm] * 2,
        out_specs=hbm,
        scratch_shapes=[
            pltpu.VMEM((columns, 16, LANES), BF16),
            pltpu.VMEM((columns, 16, LANES), BF16),
            pltpu.VMEM((columns * 16, LANES), F32),
            pltpu.VMEM((kinds * cells, width), BF16),
            pltpu.VMEM((FIELDS * ROWS, kinds * cells), BF16),
            pltpu.VMEM((kinds * ROWS // 3, 2 * LANES), BF16),
            pltpu.VMEM((2 * LANES, FIELDS * cells), BF16),
            pltpu.VMEM((2, FIELDS * ROWS, width // 2), F32),
            pltpu.VMEM((2, FIELDS * ROWS, width // 2), F32),
            pltpu.VMEM((8, ROWS, WIDTH), F32),
            pltpu.VMEM((STEPS + 1, BLOCKS, TILES, LANES), F32),
            pltpu.VMEM((BLOCKS, TILES, LANES), F32),
            pltpu.VMEM((6, BLOCKS, TILES, LANES), F32),
            pltpu.VMEM((2, 2, GROUP, 8, LANES), F32),
            pltpu.VMEM((2, 2, GROUP, 8, LANES), F32),
            dma((2,)),
            dma,
            dma,
            dma,
            dma((2,)),
            dma((2,)),
            dma((4,)),
            dma((4,)),
            dma((4,)),
            dma((4,)),
        ],
        compiler_params=pltpu.CompilerParams(
            collective_id=0, has_side_effects=True, vmem_limit_bytes=48 * 1024 * 1024
        ),
    )(
        profiles,
        lists(intersection),
        lists(weight_index),
        lists(target_row),
        atm_flux.reshape(per_device, FIELDS * cells),
        land_mask,
        state.reshape(8, ROWS, WIDTH),
        remap_weights.reshape(kinds * cells, width),
    )
    return out.reshape(state.shape)


def solution(mesh):
    in_specs = (
        P(None, "lev", "row", "col"),
        P("row", "lev", "col", None),
        P("row", "lev", "col", None),
        P("row", "lev", "col", None),
        P("row", "lev", "col", None),
        P(),
        P("row", "col"),
        P(None, "lev"),
    )
    out_specs = P(None, "lev", "row", "col")
    return jax.shard_map(local, mesh=mesh, in_specs=in_specs, out_specs=out_specs, check_vma=False)
```

```python
import functools
import math

import jax
import jax.numpy as jnp
from jax import lax
from jax.experimental import pallas as pl
from jax.experimental.pallas import tpu as pltpu
from jax.sharding import PartitionSpec as P

STEPS = 4
DIFFUSE = 0.2
SPEED = 0.3
FORCE_STEP = 0.25

MESH = pl.DeviceIdType.MESH
F32 = jnp.float32
BF16 = jnp.bfloat16
I32 = jnp.int32

CAP = 3
FIELDS = 4
SLOT = 64
ROWS = 64
WIDTH = 512
LANES = 128
BLOCKS = WIDTH // LANES
PAD = 8
EXT = ROWS + 2 * PAD
GROUP = EXT // 16
TILES = EXT * 8
HALO = STEPS


def row_of(ref, xb, r):
    if not isinstance(r, int):
        r = pl.multiple_of(r * 8, 8)
    else:
        r = r * 8
    return ref[xb, pl.ds(r, 8), :]


def far_first(col, columns):
    side = math.isqrt(columns)

    def hops(offset):
        return sum(min(part, side - part) for part in divmod(offset, side))

    return [
        lax.rem(col // side + offset // side, side) * side + lax.rem(col % side + offset % side, side)
        for offset in sorted(range(1, columns), key=lambda offset: (-hops(offset), -offset))
    ]


def kernel(
    sizes,
    prof_ref,
    dest_hbm,
    widx_hbm,
    trow_hbm,
    flux_hbm,
    mask_hbm,
    state_ref,
    weights_ref,
    out_ref,
    pairs,
    flux_ref,
    mask_ref,
    send,
    got,
    stage,
    wv,
    lhs,
    hot,
    slots,
    mine,
    theirs,
    nat,
    cells,
    force,
    coef,
    own,
    other,
    load_sem,
    out_sem,
    a2a_send,
    a2a_recv,
    lev_send,
    lev_recv,
    row_send,
    row_recv,
    col_send,
    col_recv,
):
    columns, bands = sizes
    col = lax.axis_index("col")
    row = lax.axis_index("row")
    lev = lax.axis_index("lev")
    west = lax.rem(col + columns - 1, columns)
    east = lax.rem(col + 1, columns)
    south = lax.rem(row + bands - 1, bands)
    north = lax.rem(row + 1, bands)

    state_copy = pltpu.make_async_copy(state_ref, nat, load_sem.at[0])
    weights_copy = pltpu.make_async_copy(weights_ref, wv, load_sem.at[1])
    pair_copies = [
        pltpu.make_async_copy(ref, pairs.at[i], load_sem.at[2 + i])
        for i, ref in enumerate((dest_hbm, widx_hbm, trow_hbm))
    ]
    flux_copy = pltpu.make_async_copy(flux_hbm, flux_ref, load_sem.at[5])
    mask_copy = pltpu.make_async_copy(mask_hbm, mask_ref, load_sem.at[6])
    for copy in pair_copies + [flux_copy, state_copy, weights_copy, mask_copy]:
        copy.start()

    barrier = pltpu.get_barrier_semaphore()

    peers = far_first(col, columns)
    for peer in peers:
        pl.semaphore_signal(barrier, inc=1, device_id={"col": peer}, device_id_type=MESH)
    pl.semaphore_signal(barrier, inc=1, device_id={"row": south}, device_id_type=MESH)
    pl.semaphore_signal(barrier, inc=1, device_id={"row": north}, device_id_type=MESH)
    pl.semaphore_signal(barrier, inc=1, device_id={"lev": 1 - lev}, device_id_type=MESH)

    for copy in pair_copies:
        copy.wait()
    flux_copy.wait()
    blocks = pairs.shape[2]
    dest, kind, goal = pairs[0], pairs[1], pairs[2]
    to = lax.broadcasted_iota(I32, (columns, blocks), 0)
    first = dest[0:1, :] == to
    second = dest[1:2, :] == to
    named = (first | second).astype(F32)
    before = (
        lax.broadcasted_iota(I32, (blocks, blocks), 0)
        < lax.broadcasted_iota(I32, (blocks, blocks), 1)
    ).astype(F32)
    rank = jnp.dot(named.astype(BF16), before.astype(BF16), preferred_element_type=F32)
    y_one = jnp.where(first, goal[0:1, :], goal[1:2, :]).astype(F32) + 1.0
    w_val = jnp.where(first, kind[0:1, :], kind[1:2, :]).astype(F32)
    spot = lax.broadcasted_iota(I32, (blocks, LANES), 1)
    at_y = (spot == col).astype(BF16)
    at_w = (spot == col + SLOT).astype(BF16)
    flux = flux_ref[...]
    for k in range(CAP):
        pick = jnp.where(rank == float(k), named, 0.0)
        moved = jnp.dot(pick.astype(BF16), flux, preferred_element_type=F32)
        for f in range(FIELDS):
            stage[pl.ds(k * FIELDS + f, columns, stride=16), :] = moved[:, f * LANES : (f + 1) * LANES]
        tags = jnp.dot((pick * y_one).astype(BF16), at_y, preferred_element_type=F32) + jnp.dot(
            (pick * w_val).astype(BF16), at_w, preferred_element_type=F32
        )
        stage[pl.ds(CAP * FIELDS + k, columns, stride=16), :] = tags
    stage[pl.ds(15, columns, stride=16), :] = jnp.zeros((columns, LANES), F32)
    send[...] = stage[...].astype(BF16).reshape(columns, 16, LANES)

    pl.semaphore_wait(barrier, columns + 2)

    for peer in peers:
        pltpu.make_async_remote_copy(
            src_ref=send.at[peer],
            dst_ref=got.at[col],
            send_sem=a2a_send,
            recv_sem=a2a_recv,
            device_id={"col": peer},
            device_id_type=MESH,
        ).start()
    got[pl.ds(col, 1)] = send[pl.ds(col, 1)]

    zero_rows = jnp.zeros((BLOCKS, PAD * 8, LANES), F32)
    spare = (PAD - HALO) * 8
    for ref in (cells[0], force):
        ref[:, 0:spare, :] = zero_rows[:, :spare]
        ref[:, TILES - spare : TILES, :] = zero_rows[:, :spare]
    force[:, PAD * 8 : (PAD + ROWS) * 8, :] = jnp.zeros((BLOCKS, ROWS * 8, LANES), F32)
    state_copy.wait()
    for xb in range(BLOCKS):
        for t in range(8):
            cells[0][xb, pl.ds(PAD * 8 + t, ROWS, stride=8), :] = nat[t, :, xb * LANES : (xb + 1) * LANES]

    def row_copies(ref, tag, count):
        rows = count * 8
        to_north = pltpu.make_async_remote_copy(
            src_ref=ref.at[:, pl.ds((PAD + ROWS) * 8 - rows, rows), :],
            dst_ref=ref.at[:, pl.ds(PAD * 8 - rows, rows), :],
            send_sem=row_send.at[2 * tag],
            recv_sem=row_recv.at[2 * tag],
            device_id={"row": north},
            device_id_type=MESH,
        )
        to_south = pltpu.make_async_remote_copy(
            src_ref=ref.at[:, pl.ds(PAD * 8, rows), :],
            dst_ref=ref.at[:, pl.ds((PAD + ROWS) * 8, rows), :],
            send_sem=row_send.at[2 * tag + 1],
            recv_sem=row_recv.at[2 * tag + 1],
            device_id={"row": south},
            device_id_type=MESH,
        )
        return to_north, to_south

    def settle_rows(ref, copies):
        for copy in copies:
            copy.wait()

        @pl.when(row == 0)
        def _():
            ref[:, 0 : PAD * 8, :] = zero_rows

        @pl.when(row == bands - 1)
        def _():
            ref[:, (PAD + ROWS) * 8 : TILES, :] = zero_rows

    group = lax.broadcasted_iota(I32, (8, LANES), 1) // 8

    def pack(ref, tag):
        def one(j, carry):
            left = row_of(ref, 0, j)
            right = pltpu.roll(row_of(ref, BLOCKS - 1, j), 8, 1)
            for g in range(1, 16):
                r = g * GROUP + j
                left = jnp.where(group == g, pltpu.roll(row_of(ref, 0, r), 8 * g, 1), left)
                turned = row_of(ref, BLOCKS - 1, r)
                if g < 15:
                    turned = pltpu.roll(turned, 8 * g + 8, 1)
                right = jnp.where(group == g, turned, right)
            own[tag, 0, j] = left
            own[tag, 1, j] = right
            return carry

        lax.fori_loop(0, GROUP, one, 0)

    def col_copies(tag):
        to_west = pltpu.make_async_remote_copy(
            src_ref=own.at[tag, 0],
            dst_ref=other.at[tag, 1],
            send_sem=col_send.at[2 * tag],
            recv_sem=col_recv.at[2 * tag],
            device_id={"col": west},
            device_id_type=MESH,
        )
        to_east = pltpu.make_async_remote_copy(
            src_ref=own.at[tag, 1],
            dst_ref=other.at[tag, 0],
            send_sem=col_send.at[2 * tag + 1],
            recv_sem=col_recv.at[2 * tag + 1],
            device_id={"col": east},
            device_id_type=MESH,
        )
        return to_west, to_east

    def settle_cols(tag, copies):
        for copy in copies:
            copy.wait()

        @pl.when(col == 0)
        def _():
            other[tag, 0] = jnp.zeros((GROUP, 8, LANES), F32)

        @pl.when(col == columns - 1)
        def _():
            other[tag, 1] = jnp.zeros((GROUP, 8, LANES), F32)

    state_rows = row_copies(cells[0], 0, HALO)
    for copy in state_rows:
        copy.start()
    settle_rows(cells[0], state_rows)
    pack(cells[0], 0)
    state_cols = col_copies(0)
    for copy in state_cols:
        copy.start()
    settle_cols(0, state_cols)

    everyone = pltpu.make_async_remote_copy(
        src_ref=send.at[pl.ds(0, columns - 1)],
        dst_ref=got.at[pl.ds(0, columns - 1)],
        send_sem=a2a_send,
        recv_sem=a2a_recv,
        device_id={"col": east},
        device_id_type=MESH,
    )
    everyone.wait_recv()
    stage[...] = got[...].reshape(columns * 16, LANES).astype(F32)
    lane = lax.broadcasted_iota(I32, (1, LANES), 1)
    slots[...] = jnp.zeros_like(slots)
    bins = []
    for k in range(CAP):
        for f in range(FIELDS):
            slots[k * SLOT : k * SLOT + columns, f * LANES : (f + 1) * LANES] = stage[
                pl.ds(k * FIELDS + f, columns, stride=16), :
            ].astype(BF16)
        tags = jnp.sum(stage[pl.ds(CAP * FIELDS + k, columns, stride=16), :], axis=0, keepdims=True)
        y = tags.astype(I32) - 1
        w = pltpu.roll(tags, SLOT, 1).astype(I32)
        bins.append(jnp.where((y >= 0) & (lane < SLOT), w * ROWS + y, -1))
    low = jnp.where(lane < SLOT, bins[0], pltpu.roll(bins[1], SLOT, 1))
    bin_row = jnp.concatenate([low, bins[2]], axis=1)
    kinds = lhs.shape[1] // LANES
    batch = kinds * ROWS // 3
    for part in range(3):
        index = lax.broadcasted_iota(I32, (batch, 2 * LANES), 0) + part * batch
        hot[...] = jnp.where(index == bin_row, 1.0, 0.0).astype(BF16)
        summed = jnp.dot(hot[...], slots[...], preferred_element_type=F32).astype(BF16)
        for i in range(batch // ROWS):
            w = part * (batch // ROWS) + i
            for f in range(FIELDS):
                lhs[f * ROWS : (f + 1) * ROWS, w * LANES : (w + 1) * LANES] = summed[
                    i * ROWS : (i + 1) * ROWS, f * LANES : (f + 1) * LANES
                ]
    weights_copy.wait()
    swaps = []

    def swap(source, target, half):
        return pltpu.make_async_remote_copy(
            src_ref=source,
            dst_ref=target,
            send_sem=lev_send.at[half],
            recv_sem=lev_recv.at[half],
            device_id={"lev": 1 - lev},
            device_id_type=MESH,
        )

    for half in range(2):
        mine[half] = jnp.dot(
            lhs[...], wv[:, half * 256 : (half + 1) * 256], preferred_element_type=F32
        )
        for f in range(FIELDS):
            part = pl.ds(f * ROWS, ROWS)
            swap(mine.at[half, part], theirs.at[half, part], half).start()
        swaps.append(swap(mine.at[half], theirs.at[half], half))

    mask_copy.wait()
    for half in range(2):
        swaps[half].wait()
        for inner in range(2):
            xb = 2 * half + inner
            here = slice(inner * LANES, (inner + 1) * LANES)
            wet = mask_ref[:, xb * LANES : (xb + 1) * LANES] == 1
            total = [
                mine[half, f * ROWS : (f + 1) * ROWS, here]
                + theirs[half, f * ROWS : (f + 1) * ROWS, here]
                for f in range(FIELDS)
            ]
            terms = [
                FORCE_STEP * total[0],
                FORCE_STEP * total[1],
                (0.5 * SPEED) * jnp.tanh(total[2]),
                (0.5 * SPEED) * jnp.tanh(total[3]),
                jnp.full((ROWS, LANES), DIFFUSE, F32),
            ]
            for f, term in enumerate(terms):
                force[xb, pl.ds(PAD * 8 + f, ROWS, stride=8), :] = jnp.where(wet, term, 0.0)
    force_rows = row_copies(force, 1, HALO)
    for copy in force_rows:
        copy.start()

    tracer = lax.broadcasted_iota(I32, (8, LANES), 0)

    def profile(index, keep):
        value = jnp.zeros((8, LANES), F32)
        for level in range(4):
            value = jnp.where(
                (lax.rem(tracer, 4) == level) & keep, prof_ref[index, level], value
            )
        return value

    heat = profile(0, tracer < 4)
    fresh = profile(1, tracer >= 4)
    decay = profile(2, tracer >= 0)

    def factors(term):
        spread = [jnp.broadcast_to(term(f), (8, LANES)) for f in range(5)]
        source = spread[0] * heat + spread[1] * fresh
        a = spread[2] * decay
        b = spread[3] * decay
        d = spread[4]
        return 1.0 - 4.0 * d, d - a, d + a, d - b, d + b, source

    lanes = lax.broadcasted_iota(I32, (8, LANES), 1)

    def sides(cur):
        back = [pltpu.roll(c, 1, 1) for c in cur]
        ahead = [pltpu.roll(c, LANES - 1, 1) for c in cur]
        from_west = [jnp.where(lanes == 0, back[xb - 1], back[xb]) for xb in range(BLOCKS)]
        from_east = [
            jnp.where(lanes == LANES - 1, ahead[(xb + 1) % BLOCKS], ahead[xb])
            for xb in range(BLOCKS)
        ]
        return from_west, from_east

    def combine(c, below, cur, above, left, right):
        return (
            (c[0] * cur + c[5]) + (c[1] * right + c[2] * left) + (c[3] * above + c[4] * below)
        )

    def update_rows(step, base, count, make):
        table = [
            [row_of(cells[step], xb, base + q) for xb in range(BLOCKS)] for q in range(-1, count + 1)
        ]
        results = []
        for q in range(count):
            below, cur, above = table[q : q + 3]
            left, right = sides(cur)
            at = pl.ds((base + q) * 8, 8)
            for xb in range(BLOCKS):
                if make:
                    c = factors(lambda f: force[xb, pl.ds((base + q) * 8 + f, 1), :])
                    for i in range(6):
                        coef[i, xb, at, :] = c[i]
                else:
                    c = [coef[i, xb, at, :] for i in range(6)]
                results.append(
                    (xb, at, combine(c, below[xb], cur[xb], above[xb], left[xb], right[xb]))
                )
        for xb, at, value in results:
            cells[step + 1][xb, at, :] = value

    def sweep(step, low_row, count, make):
        for start in range(0, count, 4):
            update_rows(step, low_row + start, min(4, count - start), make)

    sweep(0, PAD, ROWS, True)
    settle_rows(force, force_rows)
    pack(force, 1)
    force_cols = col_copies(1)
    for copy in force_cols:
        copy.start()
    for step in range(1, STEPS):
        sweep(step, PAD + step, ROWS - 2 * step, False)
    for step in range(STEPS):
        for base in (PAD - (STEPS - 1 - step), PAD + ROWS - step):
            update_rows(step, base, STEPS - 1, step == 0)
    last = cells[STEPS]

    def results(low, high, sem):
        for t in range(8):
            for xb in range(low, high):
                nat[t, :, xb * LANES : (xb + 1) * LANES] = last[xb, pl.ds(PAD * 8 + t, ROWS, stride=8), :]
        part = pl.ds(low * LANES, (high - low) * LANES)
        copy = pltpu.make_async_copy(nat.at[:, :, part], out_ref.at[:, :, part], sem)
        copy.start()
        return copy

    inner = results(1, BLOCKS - 1, out_sem.at[0])
    settle_cols(1, force_cols)

    spot8 = lax.rem(lax.broadcasted_iota(I32, (GROUP, 8, LANES), 2), 8)

    def strip_factors(ref):
        parts = [factors(lambda f: ref[j, f : f + 1, :]) for j in range(GROUP)]
        return [jnp.stack([p[i] for p in parts]) for i in range(6)]

    def turn(x, shift):
        return pltpu.roll(x, shift % LANES, 2)

    def strip(lefts, rights):
        (l_cells, l_force), (r_cells, r_force) = lefts, rights
        pair = [l_cells[...], r_cells[...]]
        cs = [strip_factors(l_force), strip_factors(r_force)]
        for _ in range(STEPS):
            rolled = []
            for side in range(2):
                x = pair[side]
                above = jnp.concatenate([x[1:], turn(x[:1], -8)], axis=0)
                below = jnp.concatenate([turn(x[-1:], 8), x[:-1]], axis=0)
                right, left = turn(x, -1), turn(x, 1)
                if side == 0:
                    right = jnp.where(spot8 == 7, turn(pair[1], 7), right)
                else:
                    left = jnp.where(spot8 == 0, turn(pair[0], -7), left)
                rolled.append(combine(cs[side], below, x, above, left, right))
            pair = rolled
        return pair

    own[0, 0] = strip((other.at[0, 0], other.at[1, 0]), (own.at[0, 0], own.at[1, 0]))[1]
    own[0, 1] = strip((own.at[0, 1], own.at[1, 1]), (other.at[0, 1], other.at[1, 1]))[0]
    for r in range(PAD, PAD + ROWS):
        g, j = r // GROUP, r % GROUP
        at = pl.ds(r * 8, 8)
        last[0, at, :] = jnp.where(lanes < 4, pltpu.roll(own[0, 0, j], (LANES - 8 * g) % LANES, 1), last[0, at, :])
        last[BLOCKS - 1, at, :] = jnp.where(
            lanes >= LANES - 4,
            pltpu.roll(own[0, 1, j], (LANES - 8 - 8 * g) % LANES, 1),
            last[BLOCKS - 1, at, :],
        )
    outer = [results(0, 1, out_sem.at[1]), results(BLOCKS - 1, BLOCKS, out_sem.at[2])]
    for copy in [inner] + outer:
        copy.wait()
    everyone.wait_send()


def local(
    state, atm_flux, intersection, weight_index, target_row, remap_weights, land_mask, profiles
):
    columns, bands = lax.axis_size("col"), lax.axis_size("row")
    per_device = atm_flux.shape[2]
    kinds, cells, width = remap_weights.shape

    def lists(x):
        return x.reshape(per_device, 2).T

    hbm = pl.BlockSpec(memory_space=pl.ANY)
    dma = pltpu.SemaphoreType.DMA
    out = pl.pallas_call(
        functools.partial(kernel, (columns, bands)),
        out_shape=jax.ShapeDtypeStruct((8, ROWS, WIDTH), F32),
        in_specs=[pl.BlockSpec(memory_space=pltpu.SMEM)] + [hbm] * 7,
        out_specs=hbm,
        scratch_shapes=[
            pltpu.VMEM((3, 2, per_device), I32),
            pltpu.VMEM((per_device, FIELDS * cells), BF16),
            pltpu.VMEM((ROWS, WIDTH), I32),
            pltpu.VMEM((columns, 16, LANES), BF16),
            pltpu.VMEM((columns, 16, LANES), BF16),
            pltpu.VMEM((columns * 16, LANES), F32),
            pltpu.VMEM((kinds * cells, width), BF16),
            pltpu.VMEM((FIELDS * ROWS, kinds * cells), BF16),
            pltpu.VMEM((kinds * ROWS // 3, 2 * LANES), BF16),
            pltpu.VMEM((2 * LANES, FIELDS * cells), BF16),
            pltpu.VMEM((2, FIELDS * ROWS, width // 2), F32),
            pltpu.VMEM((2, FIELDS * ROWS, width // 2), F32),
            pltpu.VMEM((8, ROWS, WIDTH), F32),
            [pltpu.VMEM((BLOCKS, TILES, LANES), F32)] * (STEPS + 1),
            pltpu.VMEM((BLOCKS, TILES, LANES), F32),
            pltpu.VMEM((6, BLOCKS, TILES, LANES), F32),
            pltpu.VMEM((2, 2, GROUP, 8, LANES), F32),
            pltpu.VMEM((2, 2, GROUP, 8, LANES), F32),
            dma((7,)),
            dma((3,)),
            dma,
            dma,
            dma((2,)),
            dma((2,)),
            dma((4,)),
            dma((4,)),
            dma((4,)),
            dma((4,)),
        ],
        compiler_params=pltpu.CompilerParams(
            collective_id=0, has_side_effects=True, vmem_limit_bytes=62 * 1024 * 1024
        ),
    )(
        profiles,
        lists(intersection),
        lists(weight_index),
        lists(target_row),
        atm_flux.reshape(per_device, FIELDS * cells),
        land_mask,
        state.reshape(8, ROWS, WIDTH),
        remap_weights.reshape(kinds * cells, width),
    )
    return out.reshape(state.shape)


def solution(mesh):
    in_specs = (
        P(None, "lev", "row", "col"),
        P("row", "lev", "col", None),
        P("row", "lev", "col", None),
        P("row", "lev", "col", None),
        P("row", "lev", "col", None),
        P(),
        P("row", "col"),
        P(None, "lev"),
    )
    out_specs = P(None, "lev", "row", "col")
    return jax.shard_map(local, mesh=mesh, in_specs=in_specs, out_specs=out_specs, check_vma=False)
```

```python
import functools
import math

import jax
import jax.numpy as jnp
from jax import lax
from jax.experimental import pallas as pl
from jax.experimental.pallas import tpu as pltpu
from jax.sharding import PartitionSpec as P

STEPS = 4
DIFFUSE = 0.2
SPEED = 0.3
FORCE_STEP = 0.25

MESH = pl.DeviceIdType.MESH
F32 = jnp.float32
BF16 = jnp.bfloat16
I32 = jnp.int32

CAP = 3
FIELDS = 4
SLOT = 64
ROWS = 64
WIDTH = 512
LANES = 128
BLOCKS = WIDTH // LANES
PAD = 8
EXT = ROWS + 2 * PAD
GROUP = EXT // 16
TILES = EXT * 8
HALO = STEPS


def row_of(ref, xb, r):
    if not isinstance(r, int):
        r = pl.multiple_of(r * 8, 8)
    else:
        r = r * 8
    return ref[xb, pl.ds(r, 8), :]


def far_first(col, columns):
    side = math.isqrt(columns)

    def hops(offset):
        return sum(min(part, side - part) for part in divmod(offset, side))

    return [
        lax.rem(col // side + offset // side, side) * side + lax.rem(col % side + offset % side, side)
        for offset in sorted(range(1, columns), key=lambda offset: (-hops(offset), -offset))
    ]


def kernel(
    sizes,
    prof_hbm,
    dest_hbm,
    widx_hbm,
    trow_hbm,
    flux_hbm,
    mask_hbm,
    state_ref,
    weights_ref,
    out_ref,
    prof_ref,
    pairs,
    flux_ref,
    mask_ref,
    send,
    got,
    stage,
    wv,
    lhs,
    hot,
    slots,
    mine,
    twin,
    nat,
    cells,
    force,
    coef,
    own,
    other,
    load_sem,
    a2a_send,
    a2a_recv,
    lev_send,
    lev_recv,
    row_send,
    row_recv,
    col_send,
    col_recv,
):
    columns, bands = sizes
    col = lax.axis_index("col")
    row = lax.axis_index("row")
    lev = lax.axis_index("lev")
    west = lax.rem(col + columns - 1, columns)
    east = lax.rem(col + 1, columns)
    south = lax.rem(row + bands - 1, bands)
    north = lax.rem(row + 1, bands)

    state_copy = pltpu.make_async_copy(state_ref, nat, load_sem.at[0])
    weights_copy = pltpu.make_async_copy(weights_ref, wv, load_sem.at[1])
    pair_copies = [
        pltpu.make_async_copy(ref, pairs.at[i], load_sem.at[2 + i])
        for i, ref in enumerate((dest_hbm, widx_hbm, trow_hbm))
    ]
    flux_copy = pltpu.make_async_copy(flux_hbm, flux_ref, load_sem.at[5])
    mask_copy = pltpu.make_async_copy(mask_hbm, mask_ref, load_sem.at[6])
    prof_copy = pltpu.make_async_copy(prof_hbm, prof_ref, load_sem.at[7])
    for copy in pair_copies + [flux_copy, state_copy, weights_copy, mask_copy, prof_copy]:
        copy.start()

    barrier = pltpu.get_barrier_semaphore()

    peers = far_first(col, columns)
    for peer in peers:
        pl.semaphore_signal(barrier, inc=1, device_id={"col": peer}, device_id_type=MESH)
    pl.semaphore_signal(barrier, inc=1, device_id={"row": south}, device_id_type=MESH)
    pl.semaphore_signal(barrier, inc=1, device_id={"row": north}, device_id_type=MESH)
    pl.semaphore_signal(barrier, inc=1, device_id={"lev": 1 - lev}, device_id_type=MESH)

    for copy in pair_copies:
        copy.wait()
    flux_copy.wait()
    blocks = pairs.shape[2]
    dest, kind, goal = pairs[0], pairs[1], pairs[2]
    to = lax.broadcasted_iota(I32, (columns, blocks), 0)
    first = dest[0:1, :] == to
    second = dest[1:2, :] == to
    named = (first | second).astype(F32)
    before = (
        lax.broadcasted_iota(I32, (blocks, blocks), 0)
        < lax.broadcasted_iota(I32, (blocks, blocks), 1)
    ).astype(F32)
    rank = jnp.dot(named.astype(BF16), before.astype(BF16), preferred_element_type=F32)
    y_one = jnp.where(first, goal[0:1, :], goal[1:2, :]).astype(F32) + 1.0
    w_val = jnp.where(first, kind[0:1, :], kind[1:2, :]).astype(F32)
    spot = lax.broadcasted_iota(I32, (blocks, LANES), 1)
    at_y = (spot == col).astype(BF16)
    at_w = (spot == col + SLOT).astype(BF16)
    flux = flux_ref[...]
    for k in range(CAP):
        pick = jnp.where(rank == float(k), named, 0.0)
        moved = jnp.dot(pick.astype(BF16), flux, preferred_element_type=F32)
        for f in range(FIELDS):
            stage[pl.ds(k * FIELDS + f, columns, stride=16), :] = moved[:, f * LANES : (f + 1) * LANES]
        tags = jnp.dot((pick * y_one).astype(BF16), at_y, preferred_element_type=F32) + jnp.dot(
            (pick * w_val).astype(BF16), at_w, preferred_element_type=F32
        )
        stage[pl.ds(CAP * FIELDS + k, columns, stride=16), :] = tags
    stage[pl.ds(15, columns, stride=16), :] = jnp.zeros((columns, LANES), F32)
    send[...] = stage[...].astype(BF16).reshape(columns, 16, LANES)

    pl.semaphore_wait(barrier, columns + 2)

    for peer in peers:
        pltpu.make_async_remote_copy(
            src_ref=send.at[peer],
            dst_ref=got.at[col],
            send_sem=a2a_send,
            recv_sem=a2a_recv,
            device_id={"col": peer},
            device_id_type=MESH,
        ).start()
    got[pl.ds(col, 1)] = send[pl.ds(col, 1)]

    zero_rows = jnp.zeros((BLOCKS, PAD * 8, LANES), F32)
    spare = (PAD - HALO) * 8
    for ref in (cells[0], force):
        ref[:, 0:spare, :] = zero_rows[:, :spare]
        ref[:, TILES - spare : TILES, :] = zero_rows[:, :spare]
    force[:, PAD * 8 : (PAD + ROWS) * 8, :] = jnp.zeros((BLOCKS, ROWS * 8, LANES), F32)
    state_copy.wait()
    for xb in range(BLOCKS):
        for t in range(8):
            cells[0][xb, pl.ds(PAD * 8 + t, ROWS, stride=8), :] = nat[t, :, xb * LANES : (xb + 1) * LANES]

    def row_copies(ref, tag, count):
        rows = count * 8
        to_north = pltpu.make_async_remote_copy(
            src_ref=ref.at[:, pl.ds((PAD + ROWS) * 8 - rows, rows), :],
            dst_ref=ref.at[:, pl.ds(PAD * 8 - rows, rows), :],
            send_sem=row_send.at[2 * tag],
            recv_sem=row_recv.at[2 * tag],
            device_id={"row": north},
            device_id_type=MESH,
        )
        to_south = pltpu.make_async_remote_copy(
            src_ref=ref.at[:, pl.ds(PAD * 8, rows), :],
            dst_ref=ref.at[:, pl.ds((PAD + ROWS) * 8, rows), :],
            send_sem=row_send.at[2 * tag + 1],
            recv_sem=row_recv.at[2 * tag + 1],
            device_id={"row": south},
            device_id_type=MESH,
        )
        return to_north, to_south

    def settle_rows(ref, copies):
        for copy in copies:
            copy.wait()

        @pl.when(row == 0)
        def _():
            ref[:, 0 : PAD * 8, :] = zero_rows

        @pl.when(row == bands - 1)
        def _():
            ref[:, (PAD + ROWS) * 8 : TILES, :] = zero_rows

    group = lax.broadcasted_iota(I32, (8, LANES), 1) // 8

    def pack(ref, tag):
        def one(j, carry):
            left = row_of(ref, 0, j)
            right = pltpu.roll(row_of(ref, BLOCKS - 1, j), 8, 1)
            for g in range(1, 16):
                r = g * GROUP + j
                left = jnp.where(group == g, pltpu.roll(row_of(ref, 0, r), 8 * g, 1), left)
                turned = row_of(ref, BLOCKS - 1, r)
                if g < 15:
                    turned = pltpu.roll(turned, 8 * g + 8, 1)
                right = jnp.where(group == g, turned, right)
            own[tag, 0, j] = left
            own[tag, 1, j] = right
            return carry

        lax.fori_loop(0, GROUP, one, 0)

    def col_copies(tag):
        to_west = pltpu.make_async_remote_copy(
            src_ref=own.at[tag, 0],
            dst_ref=other.at[tag, 1],
            send_sem=col_send.at[2 * tag],
            recv_sem=col_recv.at[2 * tag],
            device_id={"col": west},
            device_id_type=MESH,
        )
        to_east = pltpu.make_async_remote_copy(
            src_ref=own.at[tag, 1],
            dst_ref=other.at[tag, 0],
            send_sem=col_send.at[2 * tag + 1],
            recv_sem=col_recv.at[2 * tag + 1],
            device_id={"col": east},
            device_id_type=MESH,
        )
        return to_west, to_east

    def settle_cols(tag, copies):
        for copy in copies:
            copy.wait()

        @pl.when(col == 0)
        def _():
            other[tag, 0] = jnp.zeros((GROUP, 8, LANES), F32)

        @pl.when(col == columns - 1)
        def _():
            other[tag, 1] = jnp.zeros((GROUP, 8, LANES), F32)

    state_rows = row_copies(cells[0], 0, HALO)
    for copy in state_rows:
        copy.start()
    settle_rows(cells[0], state_rows)
    pack(cells[0], 0)
    state_cols = col_copies(0)
    for copy in state_cols:
        copy.start()
    settle_cols(0, state_cols)

    slots[...] = jnp.zeros_like(slots)
    everyone = pltpu.make_async_remote_copy(
        src_ref=send.at[pl.ds(0, columns - 1)],
        dst_ref=got.at[pl.ds(0, columns - 1)],
        send_sem=a2a_send,
        recv_sem=a2a_recv,
        device_id={"col": east},
        device_id_type=MESH,
    )
    everyone.wait_recv()
    relay = pltpu.make_async_remote_copy(
        src_ref=got,
        dst_ref=twin,
        send_sem=lev_send,
        recv_sem=lev_recv,
        device_id={"lev": 1 - lev},
        device_id_type=MESH,
    )
    relay.start()
    lane = lax.broadcasted_iota(I32, (1, LANES), 1)
    kinds = lhs.shape[1] // LANES
    batch = kinds * ROWS // 3

    def group_pairs(source):
        stage[...] = source[...].reshape(columns * 16, LANES).astype(F32)
        bins = []
        for k in range(CAP):
            for f in range(FIELDS):
                slots[k * SLOT : k * SLOT + columns, f * LANES : (f + 1) * LANES] = stage[
                    pl.ds(k * FIELDS + f, columns, stride=16), :
                ].astype(BF16)
            tags = jnp.sum(
                stage[pl.ds(CAP * FIELDS + k, columns, stride=16), :], axis=0, keepdims=True
            )
            y = tags.astype(I32) - 1
            w = pltpu.roll(tags, SLOT, 1).astype(I32)
            bins.append(jnp.where((y >= 0) & (lane < SLOT), w * ROWS + y, -1))
        low = jnp.where(lane < SLOT, bins[0], pltpu.roll(bins[1], SLOT, 1))
        bin_row = jnp.concatenate([low, bins[2]], axis=1)
        for part in range(3):
            index = lax.broadcasted_iota(I32, (batch, 2 * LANES), 0) + part * batch
            hot[...] = jnp.where(index == bin_row, 1.0, 0.0).astype(BF16)
            summed = jnp.dot(hot[...], slots[...], preferred_element_type=F32).astype(BF16)
            for i in range(batch // ROWS):
                w = part * (batch // ROWS) + i
                for f in range(FIELDS):
                    lhs[f * ROWS : (f + 1) * ROWS, w * LANES : (w + 1) * LANES] = summed[
                        i * ROWS : (i + 1) * ROWS, f * LANES : (f + 1) * LANES
                    ]

    group_pairs(got)
    weights_copy.wait()
    for half in range(2):
        mine[half] = jnp.dot(
            lhs[...], wv[:, half * 256 : (half + 1) * 256], preferred_element_type=F32
        )
    mask_copy.wait()
    prof_copy.wait()
    relay.wait()
    group_pairs(twin)

    for half in range(2):
        mine[half] += jnp.dot(
            lhs[...], wv[:, half * 256 : (half + 1) * 256], preferred_element_type=F32
        )
        for inner in range(2):
            xb = 2 * half + inner
            here = slice(inner * LANES, (inner + 1) * LANES)
            wet = mask_ref[:, xb * LANES : (xb + 1) * LANES] == 1
            total = [mine[half, f * ROWS : (f + 1) * ROWS, here] for f in range(FIELDS)]
            terms = [
                FORCE_STEP * total[0],
                FORCE_STEP * total[1],
                (0.5 * SPEED) * jnp.tanh(total[2]),
                (0.5 * SPEED) * jnp.tanh(total[3]),
                jnp.full((ROWS, LANES), DIFFUSE, F32),
            ]
            for f, term in enumerate(terms):
                force[xb, pl.ds(PAD * 8 + f, ROWS, stride=8), :] = jnp.where(wet, term, 0.0)
    force_rows = row_copies(force, 1, HALO)
    for copy in force_rows:
        copy.start()

    tracer = lax.broadcasted_iota(I32, (8, LANES), 0)

    def profile(index, keep):
        value = jnp.zeros((8, LANES), F32)
        for level in range(4):
            value = jnp.where(
                (lax.rem(tracer, 4) == level) & keep, prof_ref[index, level], value
            )
        return value

    heat = profile(0, tracer < 4)
    fresh = profile(1, tracer >= 4)
    decay = profile(2, tracer >= 0)

    def factors(term):
        spread = [jnp.broadcast_to(term(f), (8, LANES)) for f in range(5)]
        source = spread[0] * heat + spread[1] * fresh
        a = spread[2] * decay
        b = spread[3] * decay
        d = spread[4]
        return 1.0 - 4.0 * d, d - a, d + a, d - b, d + b, source

    lanes = lax.broadcasted_iota(I32, (8, LANES), 1)

    def sides(cur):
        back = [pltpu.roll(c, 1, 1) for c in cur]
        ahead = [pltpu.roll(c, LANES - 1, 1) for c in cur]
        from_west = [jnp.where(lanes == 0, back[xb - 1], back[xb]) for xb in range(BLOCKS)]
        from_east = [
            jnp.where(lanes == LANES - 1, ahead[(xb + 1) % BLOCKS], ahead[xb])
            for xb in range(BLOCKS)
        ]
        return from_west, from_east

    def combine(c, below, cur, above, left, right):
        return (
            (c[0] * cur + c[5]) + (c[1] * right + c[2] * left) + (c[3] * above + c[4] * below)
        )

    def update_rows(step, base, count, make):
        table = [
            [row_of(cells[step], xb, base + q) for xb in range(BLOCKS)] for q in range(-1, count + 1)
        ]
        results = []
        for q in range(count):
            below, cur, above = table[q : q + 3]
            left, right = sides(cur)
            at = pl.ds((base + q) * 8, 8)
            for xb in range(BLOCKS):
                if make:
                    c = factors(lambda f: force[xb, pl.ds((base + q) * 8 + f, 1), :])
                    for i in range(6):
                        coef[i, xb, at, :] = c[i]
                else:
                    c = [coef[i, xb, at, :] for i in range(6)]
                results.append(
                    (xb, at, combine(c, below[xb], cur[xb], above[xb], left[xb], right[xb]))
                )
        for xb, at, value in results:
            cells[step + 1][xb, at, :] = value

    def sweep(step, low_row, count, make):
        for start in range(0, count, 4):
            update_rows(step, low_row + start, min(4, count - start), make)

    sweep(0, PAD, ROWS, True)
    settle_rows(force, force_rows)
    pack(force, 1)
    force_cols = col_copies(1)
    for copy in force_cols:
        copy.start()
    for step in range(1, STEPS):
        sweep(step, PAD + step, ROWS - 2 * step, False)
    for step in range(STEPS):
        for base in (PAD - (STEPS - 1 - step), PAD + ROWS - step):
            update_rows(step, base, STEPS - 1, step == 0)
    last = cells[STEPS]

    def results(xb):
        for t in range(8):
            out_ref[t, :, xb * LANES : (xb + 1) * LANES] = last[xb, pl.ds(PAD * 8 + t, ROWS, stride=8), :]

    for xb in range(1, BLOCKS - 1):
        results(xb)
    settle_cols(1, force_cols)

    spot8 = lax.rem(lax.broadcasted_iota(I32, (GROUP, 8, LANES), 2), 8)

    def strip_factors(ref):
        parts = [factors(lambda f: ref[j, f : f + 1, :]) for j in range(GROUP)]
        return [jnp.stack([p[i] for p in parts]) for i in range(6)]

    def turn(x, shift):
        return pltpu.roll(x, shift % LANES, 2)

    def strip(lefts, rights):
        (l_cells, l_force), (r_cells, r_force) = lefts, rights
        pair = [l_cells[...], r_cells[...]]
        cs = [strip_factors(l_force), strip_factors(r_force)]
        for _ in range(STEPS):
            rolled = []
            for side in range(2):
                x = pair[side]
                above = jnp.concatenate([x[1:], turn(x[:1], -8)], axis=0)
                below = jnp.concatenate([turn(x[-1:], 8), x[:-1]], axis=0)
                right, left = turn(x, -1), turn(x, 1)
                if side == 0:
                    right = jnp.where(spot8 == 7, turn(pair[1], 7), right)
                else:
                    left = jnp.where(spot8 == 0, turn(pair[0], -7), left)
                rolled.append(combine(cs[side], below, x, above, left, right))
            pair = rolled
        return pair

    own[0, 0] = strip((other.at[0, 0], other.at[1, 0]), (own.at[0, 0], own.at[1, 0]))[1]
    own[0, 1] = strip((own.at[0, 1], own.at[1, 1]), (other.at[0, 1], other.at[1, 1]))[0]
    for r in range(PAD, PAD + ROWS):
        g, j = r // GROUP, r % GROUP
        at = pl.ds(r * 8, 8)
        last[0, at, :] = jnp.where(lanes < 4, pltpu.roll(own[0, 0, j], (LANES - 8 * g) % LANES, 1), last[0, at, :])
        last[BLOCKS - 1, at, :] = jnp.where(
            lanes >= LANES - 4,
            pltpu.roll(own[0, 1, j], (LANES - 8 - 8 * g) % LANES, 1),
            last[BLOCKS - 1, at, :],
        )
    results(0)
    results(BLOCKS - 1)
    everyone.wait_send()


def local(
    state, atm_flux, intersection, weight_index, target_row, remap_weights, land_mask, profiles
):
    columns, bands = lax.axis_size("col"), lax.axis_size("row")
    per_device = atm_flux.shape[2]
    kinds, cells, width = remap_weights.shape

    def lists(x):
        return x.reshape(per_device, 2).T

    hbm = pl.BlockSpec(memory_space=pl.ANY)
    dma = pltpu.SemaphoreType.DMA
    out = pl.pallas_call(
        functools.partial(kernel, (columns, bands)),
        out_shape=pltpu.VMEM((8, ROWS, WIDTH), F32),
        in_specs=[hbm] * 8,
        out_specs=pl.BlockSpec(memory_space=pltpu.VMEM),
        scratch_shapes=[
            pltpu.SMEM(profiles.shape, F32),
            pltpu.VMEM((3, 2, per_device), I32),
            pltpu.VMEM((per_device, FIELDS * cells), BF16),
            pltpu.VMEM((ROWS, WIDTH), I32),
            pltpu.VMEM((columns, 16, LANES), BF16),
            pltpu.VMEM((columns, 16, LANES), BF16),
            pltpu.VMEM((columns * 16, LANES), F32),
            pltpu.VMEM((kinds * cells, width), BF16),
            pltpu.VMEM((FIELDS * ROWS, kinds * cells), BF16),
            pltpu.VMEM((kinds * ROWS // 3, 2 * LANES), BF16),
            pltpu.VMEM((2 * LANES, FIELDS * cells), BF16),
            pltpu.VMEM((2, FIELDS * ROWS, width // 2), F32),
            pltpu.VMEM((columns, 16, LANES), BF16),
            pltpu.VMEM((8, ROWS, WIDTH), F32),
            [pltpu.VMEM((BLOCKS, TILES, LANES), F32)] * (STEPS + 1),
            pltpu.VMEM((BLOCKS, TILES, LANES), F32),
            pltpu.VMEM((6, BLOCKS, TILES, LANES), F32),
            pltpu.VMEM((2, 2, GROUP, 8, LANES), F32),
            pltpu.VMEM((2, 2, GROUP, 8, LANES), F32),
            dma((8,)),
            dma,
            dma,
            dma,
            dma,
            dma((4,)),
            dma((4,)),
            dma((4,)),
            dma((4,)),
        ],
        compiler_params=pltpu.CompilerParams(
            collective_id=0, has_side_effects=True, vmem_limit_bytes=48 * 1024 * 1024
        ),
    )(
        *(
            pltpu.with_memory_space_constraint(x, pltpu.HBM)
            for x in (
                profiles,
                lists(intersection),
                lists(weight_index),
                lists(target_row),
                atm_flux.reshape(per_device, FIELDS * cells),
                land_mask,
                state.reshape(8, ROWS, WIDTH),
                remap_weights.reshape(kinds * cells, width),
            )
        ),
    )
    return out.reshape(state.shape)


def solution(mesh):
    in_specs = (
        P(None, "lev", "row", "col"),
        P("row", "lev", "col", None),
        P("row", "lev", "col", None),
        P("row", "lev", "col", None),
        P("row", "lev", "col", None),
        P(),
        P("row", "col"),
        P(None, "lev"),
    )
    out_specs = P(None, "lev", "row", "col")
    return jax.shard_map(local, mesh=mesh, in_specs=in_specs, out_specs=out_specs, check_vma=False)
```

```python
import functools
import math

import jax
import jax.numpy as jnp
from jax import lax
from jax.experimental import pallas as pl
from jax.experimental.pallas import tpu as pltpu
from jax.sharding import PartitionSpec as P

STEPS = 4
DIFFUSE = 0.2
SPEED = 0.3
FORCE_STEP = 0.25

MESH = pl.DeviceIdType.MESH
F32 = jnp.float32
BF16 = jnp.bfloat16
I32 = jnp.int32

CAP = 3
FIELDS = 4
SLOT = 64
ROWS = 64
WIDTH = 512
LANES = 128
BLOCKS = WIDTH // LANES
PAD = 8
EXT = ROWS + 2 * PAD
GROUP = EXT // 16
TILES = EXT * 8
HALO = STEPS


def row_of(ref, xb, r):
    if not isinstance(r, int):
        r = pl.multiple_of(r * 8, 8)
    else:
        r = r * 8
    return ref[xb, pl.ds(r, 8), :]


def far_first(col, lev, columns):
    side = math.isqrt(columns)

    def hops(offset):
        return sum(min(part, side - part) for part in divmod(offset, side))

    x, z, way = col // side + side, col % side + side, 1 - 2 * lev
    return [
        lax.rem(x + way * (offset // side), side) * side + lax.rem(z + way * (offset % side), side)
        for offset in sorted(range(1, columns), key=lambda offset: (-hops(offset), -offset))
    ]


def kernel(
    sizes,
    prof_hbm,
    dest_hbm,
    widx_hbm,
    trow_hbm,
    flux_hbm,
    mask_hbm,
    state_ref,
    weights_ref,
    out_ref,
    prof_ref,
    pairs,
    flux_ref,
    mask_ref,
    send,
    got,
    stage,
    wv,
    lhs,
    hot,
    slots,
    mine,
    twin,
    nat,
    cells,
    force,
    coef,
    own,
    other,
    load_sem,
    a2a_send,
    a2a_recv,
    lev_send,
    lev_recv,
    row_send,
    row_recv,
    col_send,
    col_recv,
):
    columns, bands = sizes
    col = lax.axis_index("col")
    row = lax.axis_index("row")
    lev = lax.axis_index("lev")
    west = lax.rem(col + columns - 1, columns)
    east = lax.rem(col + 1, columns)
    south = lax.rem(row + bands - 1, bands)
    north = lax.rem(row + 1, bands)

    state_copy = pltpu.make_async_copy(state_ref, nat, load_sem.at[0])
    weights_copy = pltpu.make_async_copy(weights_ref, wv, load_sem.at[1])
    pair_copies = [
        pltpu.make_async_copy(ref, pairs.at[i], load_sem.at[2 + i])
        for i, ref in enumerate((dest_hbm, widx_hbm, trow_hbm))
    ]
    flux_copy = pltpu.make_async_copy(flux_hbm, flux_ref, load_sem.at[5])
    mask_copy = pltpu.make_async_copy(mask_hbm, mask_ref, load_sem.at[6])
    prof_copy = pltpu.make_async_copy(prof_hbm, prof_ref, load_sem.at[7])
    for copy in pair_copies + [flux_copy]:
        copy.start()

    barrier = pltpu.get_barrier_semaphore()

    peers = far_first(col, lev, columns)
    for peer in peers:
        pl.semaphore_signal(barrier, inc=1, device_id={"col": peer}, device_id_type=MESH)
    pl.semaphore_signal(barrier, inc=1, device_id={"row": south}, device_id_type=MESH)
    pl.semaphore_signal(barrier, inc=1, device_id={"row": north}, device_id_type=MESH)
    pl.semaphore_signal(barrier, inc=1, device_id={"lev": 1 - lev}, device_id_type=MESH)
    for copy in (state_copy, weights_copy, mask_copy, prof_copy):
        copy.start()

    for copy in pair_copies:
        copy.wait()
    flux_copy.wait()
    blocks = pairs.shape[2]
    dest, kind, goal = pairs[0], pairs[1], pairs[2]
    to = lax.broadcasted_iota(I32, (columns, blocks), 0)
    first = dest[0:1, :] == to
    second = dest[1:2, :] == to
    named = (first | second).astype(F32)
    before = (
        lax.broadcasted_iota(I32, (blocks, blocks), 0)
        < lax.broadcasted_iota(I32, (blocks, blocks), 1)
    ).astype(F32)
    rank = jnp.dot(named.astype(BF16), before.astype(BF16), preferred_element_type=F32)
    y_one = jnp.where(first, goal[0:1, :], goal[1:2, :]).astype(F32) + 1.0
    w_val = jnp.where(first, kind[0:1, :], kind[1:2, :]).astype(F32)
    spot = lax.broadcasted_iota(I32, (blocks, LANES), 1)
    at_y = (spot == col).astype(BF16)
    at_w = (spot == col + SLOT).astype(BF16)
    flux = flux_ref[...]
    for k in range(CAP):
        pick = jnp.where(rank == float(k), named, 0.0)
        moved = jnp.dot(pick.astype(BF16), flux, preferred_element_type=F32)
        for f in range(FIELDS):
            stage[pl.ds(k * FIELDS + f, columns, stride=16), :] = moved[:, f * LANES : (f + 1) * LANES]
        tags = jnp.dot((pick * y_one).astype(BF16), at_y, preferred_element_type=F32) + jnp.dot(
            (pick * w_val).astype(BF16), at_w, preferred_element_type=F32
        )
        stage[pl.ds(CAP * FIELDS + k, columns, stride=16), :] = tags
    stage[pl.ds(15, columns, stride=16), :] = jnp.zeros((columns, LANES), F32)
    send[...] = stage[...].astype(BF16).reshape(columns, 16, LANES)

    pl.semaphore_wait(barrier, columns + 2)

    for peer in peers:
        pltpu.make_async_remote_copy(
            src_ref=send.at[peer],
            dst_ref=got.at[col],
            send_sem=a2a_send,
            recv_sem=a2a_recv,
            device_id={"col": peer},
            device_id_type=MESH,
        ).start()
    got[pl.ds(col, 1)] = send[pl.ds(col, 1)]

    zero_rows = jnp.zeros((BLOCKS, PAD * 8, LANES), F32)
    spare = (PAD - HALO) * 8
    for ref in (cells[0], force):
        ref[:, 0:spare, :] = zero_rows[:, :spare]
        ref[:, TILES - spare : TILES, :] = zero_rows[:, :spare]
    force[:, PAD * 8 : (PAD + ROWS) * 8, :] = jnp.zeros((BLOCKS, ROWS * 8, LANES), F32)
    state_copy.wait()
    for xb in range(BLOCKS):
        for t in range(8):
            cells[0][xb, pl.ds(PAD * 8 + t, ROWS, stride=8), :] = nat[t, :, xb * LANES : (xb + 1) * LANES]

    def row_copies(ref, tag, count):
        rows = count * 8
        to_north = pltpu.make_async_remote_copy(
            src_ref=ref.at[:, pl.ds((PAD + ROWS) * 8 - rows, rows), :],
            dst_ref=ref.at[:, pl.ds(PAD * 8 - rows, rows), :],
            send_sem=row_send.at[2 * tag],
            recv_sem=row_recv.at[2 * tag],
            device_id={"row": north},
            device_id_type=MESH,
        )
        to_south = pltpu.make_async_remote_copy(
            src_ref=ref.at[:, pl.ds(PAD * 8, rows), :],
            dst_ref=ref.at[:, pl.ds((PAD + ROWS) * 8, rows), :],
            send_sem=row_send.at[2 * tag + 1],
            recv_sem=row_recv.at[2 * tag + 1],
            device_id={"row": south},
            device_id_type=MESH,
        )
        return to_north, to_south

    def settle_rows(ref, copies):
        for copy in copies:
            copy.wait()

        @pl.when(row == 0)
        def _():
            ref[:, 0 : PAD * 8, :] = zero_rows

        @pl.when(row == bands - 1)
        def _():
            ref[:, (PAD + ROWS) * 8 : TILES, :] = zero_rows

    group = lax.broadcasted_iota(I32, (8, LANES), 1) // 8

    def pack(ref, tag):
        def one(j, carry):
            left = row_of(ref, 0, j)
            right = pltpu.roll(row_of(ref, BLOCKS - 1, j), 8, 1)
            for g in range(1, 16):
                r = g * GROUP + j
                left = jnp.where(group == g, pltpu.roll(row_of(ref, 0, r), 8 * g, 1), left)
                turned = row_of(ref, BLOCKS - 1, r)
                if g < 15:
                    turned = pltpu.roll(turned, 8 * g + 8, 1)
                right = jnp.where(group == g, turned, right)
            own[tag, 0, j] = left
            own[tag, 1, j] = right
            return carry

        lax.fori_loop(0, GROUP, one, 0)

    def col_copies(tag):
        to_west = pltpu.make_async_remote_copy(
            src_ref=own.at[tag, 0],
            dst_ref=other.at[tag, 1],
            send_sem=col_send.at[2 * tag],
            recv_sem=col_recv.at[2 * tag],
            device_id={"col": west},
            device_id_type=MESH,
        )
        to_east = pltpu.make_async_remote_copy(
            src_ref=own.at[tag, 1],
            dst_ref=other.at[tag, 0],
            send_sem=col_send.at[2 * tag + 1],
            recv_sem=col_recv.at[2 * tag + 1],
            device_id={"col": east},
            device_id_type=MESH,
        )
        return to_west, to_east

    def settle_cols(tag, copies):
        for copy in copies:
            copy.wait()

        @pl.when(col == 0)
        def _():
            other[tag, 0] = jnp.zeros((GROUP, 8, LANES), F32)

        @pl.when(col == columns - 1)
        def _():
            other[tag, 1] = jnp.zeros((GROUP, 8, LANES), F32)

    state_rows = row_copies(cells[0], 0, HALO)
    for copy in state_rows:
        copy.start()
    settle_rows(cells[0], state_rows)
    pack(cells[0], 0)
    state_cols = col_copies(0)
    for copy in state_cols:
        copy.start()
    settle_cols(0, state_cols)

    slots[...] = jnp.zeros_like(slots)
    everyone = pltpu.make_async_remote_copy(
        src_ref=send.at[pl.ds(0, columns - 1)],
        dst_ref=got.at[pl.ds(0, columns - 1)],
        send_sem=a2a_send,
        recv_sem=a2a_recv,
        device_id={"col": east},
        device_id_type=MESH,
    )
    everyone.wait_recv()
    relay = pltpu.make_async_remote_copy(
        src_ref=got,
        dst_ref=twin,
        send_sem=lev_send,
        recv_sem=lev_recv,
        device_id={"lev": 1 - lev},
        device_id_type=MESH,
    )
    relay.start()
    lane = lax.broadcasted_iota(I32, (1, LANES), 1)
    kinds = lhs.shape[1] // LANES
    batch = kinds * ROWS // 3

    def group_pairs(source):
        stage[...] = source[...].reshape(columns * 16, LANES).astype(F32)
        bins = []
        for k in range(CAP):
            for f in range(FIELDS):
                slots[k * SLOT : k * SLOT + columns, f * LANES : (f + 1) * LANES] = stage[
                    pl.ds(k * FIELDS + f, columns, stride=16), :
                ].astype(BF16)
            tags = jnp.sum(
                stage[pl.ds(CAP * FIELDS + k, columns, stride=16), :], axis=0, keepdims=True
            )
            y = tags.astype(I32) - 1
            w = pltpu.roll(tags, SLOT, 1).astype(I32)
            bins.append(jnp.where((y >= 0) & (lane < SLOT), w * ROWS + y, -1))
        low = jnp.where(lane < SLOT, bins[0], pltpu.roll(bins[1], SLOT, 1))
        bin_row = jnp.concatenate([low, bins[2]], axis=1)
        for part in range(3):
            index = lax.broadcasted_iota(I32, (batch, 2 * LANES), 0) + part * batch
            hot[...] = jnp.where(index == bin_row, 1.0, 0.0).astype(BF16)
            summed = jnp.dot(hot[...], slots[...], preferred_element_type=F32).astype(BF16)
            for i in range(batch // ROWS):
                w = part * (batch // ROWS) + i
                for f in range(FIELDS):
                    lhs[f * ROWS : (f + 1) * ROWS, w * LANES : (w + 1) * LANES] = summed[
                        i * ROWS : (i + 1) * ROWS, f * LANES : (f + 1) * LANES
                    ]

    group_pairs(got)
    weights_copy.wait()
    for half in range(2):
        mine[half] = jnp.dot(
            lhs[...], wv[:, half * 256 : (half + 1) * 256], preferred_element_type=F32
        )
    mask_copy.wait()
    prof_copy.wait()
    relay.wait()
    group_pairs(twin)

    for half in range(2):
        mine[half] += jnp.dot(
            lhs[...], wv[:, half * 256 : (half + 1) * 256], preferred_element_type=F32
        )
        for inner in range(2):
            xb = 2 * half + inner
            here = slice(inner * LANES, (inner + 1) * LANES)
            wet = mask_ref[:, xb * LANES : (xb + 1) * LANES] == 1
            total = [mine[half, f * ROWS : (f + 1) * ROWS, here] for f in range(FIELDS)]
            terms = [
                FORCE_STEP * total[0],
                FORCE_STEP * total[1],
                (0.5 * SPEED) * jnp.tanh(total[2]),
                (0.5 * SPEED) * jnp.tanh(total[3]),
                jnp.full((ROWS, LANES), DIFFUSE, F32),
            ]
            for f, term in enumerate(terms):
                force[xb, pl.ds(PAD * 8 + f, ROWS, stride=8), :] = jnp.where(wet, term, 0.0)
    force_rows = row_copies(force, 1, HALO)
    for copy in force_rows:
        copy.start()

    tracer = lax.broadcasted_iota(I32, (8, LANES), 0)

    def profile(index, keep):
        value = jnp.zeros((8, LANES), F32)
        for level in range(4):
            value = jnp.where(
                (lax.rem(tracer, 4) == level) & keep, prof_ref[index, level], value
            )
        return value

    heat = profile(0, tracer < 4)
    fresh = profile(1, tracer >= 4)
    decay = profile(2, tracer >= 0)

    def factors(term):
        spread = [jnp.broadcast_to(term(f), (8, LANES)) for f in range(5)]
        source = spread[0] * heat + spread[1] * fresh
        a = spread[2] * decay
        b = spread[3] * decay
        d = spread[4]
        return 1.0 - 4.0 * d, d - a, d + a, d - b, d + b, source

    lanes = lax.broadcasted_iota(I32, (8, LANES), 1)

    def sides(cur):
        back = [pltpu.roll(c, 1, 1) for c in cur]
        ahead = [pltpu.roll(c, LANES - 1, 1) for c in cur]
        from_west = [jnp.where(lanes == 0, back[xb - 1], back[xb]) for xb in range(BLOCKS)]
        from_east = [
            jnp.where(lanes == LANES - 1, ahead[(xb + 1) % BLOCKS], ahead[xb])
            for xb in range(BLOCKS)
        ]
        return from_west, from_east

    def combine(c, below, cur, above, left, right):
        return (
            (c[0] * cur + c[5]) + (c[1] * right + c[2] * left) + (c[3] * above + c[4] * below)
        )

    def update_rows(step, base, count, make):
        table = [
            [row_of(cells[step], xb, base + q) for xb in range(BLOCKS)] for q in range(-1, count + 1)
        ]
        results = []
        for q in range(count):
            below, cur, above = table[q : q + 3]
            left, right = sides(cur)
            at = pl.ds((base + q) * 8, 8)
            for xb in range(BLOCKS):
                if make:
                    c = factors(lambda f: force[xb, pl.ds((base + q) * 8 + f, 1), :])
                    for i in range(6):
                        coef[i, xb, at, :] = c[i]
                else:
                    c = [coef[i, xb, at, :] for i in range(6)]
                results.append(
                    (xb, at, combine(c, below[xb], cur[xb], above[xb], left[xb], right[xb]))
                )
        for xb, at, value in results:
            cells[step + 1][xb, at, :] = value

    def sweep(step, low_row, count, make):
        for start in range(0, count, 4):
            update_rows(step, low_row + start, min(4, count - start), make)

    sweep(0, PAD, ROWS, True)
    sweep(1, PAD + 1, ROWS - 2, False)
    settle_rows(force, force_rows)
    pack(force, 1)
    force_cols = col_copies(1)
    for copy in force_cols:
        copy.start()
    for step in range(2, STEPS):
        sweep(step, PAD + step, ROWS - 2 * step, False)
    for step in range(STEPS):
        for base in (PAD - (STEPS - 1 - step), PAD + ROWS - step):
            update_rows(step, base, STEPS - 1, step == 0)
    last = cells[STEPS]

    def results(xb):
        for t in range(8):
            out_ref[t, :, xb * LANES : (xb + 1) * LANES] = last[xb, pl.ds(PAD * 8 + t, ROWS, stride=8), :]

    for xb in range(1, BLOCKS - 1):
        results(xb)
    settle_cols(1, force_cols)

    spot8 = lax.rem(lax.broadcasted_iota(I32, (GROUP, 8, LANES), 2), 8)

    def strip_factors(ref):
        parts = [factors(lambda f: ref[j, f : f + 1, :]) for j in range(GROUP)]
        return [jnp.stack([p[i] for p in parts]) for i in range(6)]

    def turn(x, shift):
        return pltpu.roll(x, shift % LANES, 2)

    def strip(lefts, rights):
        (l_cells, l_force), (r_cells, r_force) = lefts, rights
        pair = [l_cells[...], r_cells[...]]
        cs = [strip_factors(l_force), strip_factors(r_force)]
        for _ in range(STEPS):
            rolled = []
            for side in range(2):
                x = pair[side]
                above = jnp.concatenate([x[1:], turn(x[:1], -8)], axis=0)
                below = jnp.concatenate([turn(x[-1:], 8), x[:-1]], axis=0)
                right, left = turn(x, -1), turn(x, 1)
                if side == 0:
                    right = jnp.where(spot8 == 7, turn(pair[1], 7), right)
                else:
                    left = jnp.where(spot8 == 0, turn(pair[0], -7), left)
                rolled.append(combine(cs[side], below, x, above, left, right))
            pair = rolled
        return pair

    own[0, 0] = strip((other.at[0, 0], other.at[1, 0]), (own.at[0, 0], own.at[1, 0]))[1]
    own[0, 1] = strip((own.at[0, 1], own.at[1, 1]), (other.at[0, 1], other.at[1, 1]))[0]
    for r in range(PAD, PAD + ROWS):
        g, j = r // GROUP, r % GROUP
        at = pl.ds(r * 8, 8)
        last[0, at, :] = jnp.where(lanes < 4, pltpu.roll(own[0, 0, j], (LANES - 8 * g) % LANES, 1), last[0, at, :])
        last[BLOCKS - 1, at, :] = jnp.where(
            lanes >= LANES - 4,
            pltpu.roll(own[0, 1, j], (LANES - 8 - 8 * g) % LANES, 1),
            last[BLOCKS - 1, at, :],
        )
    results(0)
    results(BLOCKS - 1)
    everyone.wait_send()


def local(
    state, atm_flux, intersection, weight_index, target_row, remap_weights, land_mask, profiles
):
    columns, bands = lax.axis_size("col"), lax.axis_size("row")
    per_device = atm_flux.shape[2]
    kinds, cells, width = remap_weights.shape

    def lists(x):
        return x.reshape(per_device, 2).T

    hbm = pl.BlockSpec(memory_space=pl.ANY)
    dma = pltpu.SemaphoreType.DMA
    out = pl.pallas_call(
        functools.partial(kernel, (columns, bands)),
        out_shape=pltpu.VMEM((8, ROWS, WIDTH), F32),
        in_specs=[hbm] * 8,
        out_specs=pl.BlockSpec(memory_space=pltpu.VMEM),
        scratch_shapes=[
            pltpu.SMEM(profiles.shape, F32),
            pltpu.VMEM((3, 2, per_device), I32),
            pltpu.VMEM((per_device, FIELDS * cells), BF16),
            pltpu.VMEM((ROWS, WIDTH), I32),
            pltpu.VMEM((columns, 16, LANES), BF16),
            pltpu.VMEM((columns, 16, LANES), BF16),
            pltpu.VMEM((columns * 16, LANES), F32),
            pltpu.VMEM((kinds * cells, width), BF16),
            pltpu.VMEM((FIELDS * ROWS, kinds * cells), BF16),
            pltpu.VMEM((kinds * ROWS // 3, 2 * LANES), BF16),
            pltpu.VMEM((2 * LANES, FIELDS * cells), BF16),
            pltpu.VMEM((2, FIELDS * ROWS, width // 2), F32),
            pltpu.VMEM((columns, 16, LANES), BF16),
            pltpu.VMEM((8, ROWS, WIDTH), F32),
            [pltpu.VMEM((BLOCKS, TILES, LANES), F32)] * (STEPS + 1),
            pltpu.VMEM((BLOCKS, TILES, LANES), F32),
            pltpu.VMEM((6, BLOCKS, TILES, LANES), F32),
            pltpu.VMEM((2, 2, GROUP, 8, LANES), F32),
            pltpu.VMEM((2, 2, GROUP, 8, LANES), F32),
            dma((8,)),
            dma,
            dma,
            dma,
            dma,
            dma((4,)),
            dma((4,)),
            dma((4,)),
            dma((4,)),
        ],
        compiler_params=pltpu.CompilerParams(
            collective_id=0, has_side_effects=True, vmem_limit_bytes=48 * 1024 * 1024
        ),
    )(
        *(
            pltpu.with_memory_space_constraint(x, pltpu.HBM)
            for x in (
                profiles,
                lists(intersection),
                lists(weight_index),
                lists(target_row),
                atm_flux.reshape(per_device, FIELDS * cells),
                land_mask,
                state.reshape(8, ROWS, WIDTH),
                remap_weights.reshape(kinds * cells, width),
            )
        ),
    )
    return out.reshape(state.shape)


def solution(mesh):
    in_specs = (
        P(None, "lev", "row", "col"),
        P("row", "lev", "col", None),
        P("row", "lev", "col", None),
        P("row", "lev", "col", None),
        P("row", "lev", "col", None),
        P(),
        P("row", "col"),
        P(None, "lev"),
    )
    out_specs = P(None, "lev", "row", "col")
    return jax.shard_map(local, mesh=mesh, in_specs=in_specs, out_specs=out_specs, check_vma=False)
```
